256 devices in a mesh: snp: 64 (over y, z, core), smp: 4 (over x).
Axes of the slice: x: 4, y: 4, z: 8, core: 2. Of those that a mesh axis runs over, the one named last changes fastest.
Arguments:
- dosages: bfloat16 [65536, 8192], P('snp', 'smp'), may hold values from -6 to 6
- reach: int32 [128], replicated, may hold values from 0 to 6, as said below
- counts: int32 [65536], replicated, may hold values from 4096 to 8192
Outputs:
- ld_tiles: float32 [128, 7, 512, 512], P('snp', None, 'smp')
The draws below stay inside these ranges and needn't reach their ends.
Inputs may be any that keep to these rules, and one draw needn't show every extreme that they name: reach[b] <= min(6, 127 - b); reach[0] = 6.
All inputs are finite; a program needn't handle non-finite values.
Results may differ from the reference program's by a relative error of at most 0.0003.
Values may be sent and summed in bfloat16 or wider, within the bound.
No kernel may reach another device: no remote copies, remote signals or barrier semaphores. Data moves between devices by JAX's collectives and lax.ppermute only.
A program may use at most 128 MiB of HBM per device.

```python
import jax
import jax.numpy as jnp
from jax import lax

BLOCK = 512
REACH_MAX = 6
SMP_DEV = 2048
NBLK = 128
SNPS = 65536
SAMPLES = 8192
N_SMP = 4


def draw_reach(key, part):
    raw = jax.random.randint(key, (NBLK,), 1, REACH_MAX + 1)
    raw = raw.at[0].set(REACH_MAX)
    limit = NBLK - 1 - jnp.arange(NBLK, dtype=jnp.int32)
    return jnp.minimum(raw, limit).astype(jnp.int32)


def touch_ends(entries, key, smallest, high):
    shape = entries.shape
    spot = [jax.random.randint(jax.random.fold_in(key, axis), (), 0, shape[axis]) for axis in range(len(shape))]
    entries = entries.at[tuple(spot)].set(smallest)
    longest = shape.index(max(shape))
    spot[longest] = (spot[longest] + 1) % shape[longest]
    return entries.at[tuple(spot)].set(high)


def level_of(key, shape, split, least, largest):
    def one(position, blocks):
        draws = jax.random.uniform(jax.random.fold_in(jax.random.fold_in(key, 6), position), (blocks,), jnp.float32, least / len(split), largest / len(split))
        return jnp.repeat(jnp.exp(draws), shape[position] // blocks).reshape((-1,) + (1,) * (len(shape) - position - 1))

    level = one(*split[0])
    for cut in split[1:]:
        level = level * one(*cut)
    return level


def normal_values(key, extent, scale, most, split=(), held_as=jnp.bfloat16):
    values = scale * jax.random.normal(key, extent, jnp.float32)
    if split:
        values = values * level_of(key, extent, split, -0.22, 0.18)
    return jnp.clip(values, -most, most).astype(held_as)


def setup_inputs(seed: int = 0) -> dict:
    streams_of = jax.random.split(jax.random.key(seed), 4)
    return {
        "dosages": normal_values(streams_of[0], (SNPS, SAMPLES), 1.0, 6.0, ((0, 64), (1, 4))),
        "reach": draw_reach(jax.random.fold_in(streams_of[3], 71), 0),
        "counts": touch_ends(jax.random.randint(streams_of[2], (SNPS,), SAMPLES // 2, SAMPLES + 1), jax.random.fold_in(streams_of[2], 1), SAMPLES // 2, SAMPLES).astype(jnp.int32),
    }


def reference(dosages, reach, counts):
    snps = dosages.shape[0]
    nblocks = snps // BLOCK
    width = (REACH_MAX + 1) * BLOCK
    padded = jnp.concatenate([dosages, jnp.zeros((REACH_MAX * BLOCK, dosages.shape[1]), jnp.bfloat16)], 0)
    inv_all = lax.rsqrt(counts.astype(jnp.float32))
    inv_pad = jnp.concatenate([inv_all, jnp.ones((REACH_MAX * BLOCK,), jnp.float32)], 0)
    offsets = jnp.arange(REACH_MAX + 1, dtype=jnp.int32)

    def one_block(block_index):
        start = (block_index * BLOCK).astype(jnp.int32)
        row_block = lax.dynamic_slice_in_dim(padded, start, BLOCK, 0)
        col_block = lax.dynamic_slice_in_dim(padded, start, width, 0)
        row_groups = row_block.reshape(BLOCK, N_SMP, SMP_DEV).astype(jnp.float32)
        col_groups = col_block.reshape(width, N_SMP, SMP_DEV).astype(jnp.float32)
        partial_value = jnp.einsum('pcs,qcs->cpq', row_groups, col_groups, precision=lax.Precision.HIGHEST)
        gram = lax.optimization_barrier(jnp.sum(partial_value, axis=0))
        gram = gram.reshape(BLOCK, REACH_MAX + 1, BLOCK).transpose(1, 0, 2)
        inv_rows = lax.dynamic_slice_in_dim(inv_pad, start, BLOCK, 0)
        inv_cols = lax.dynamic_slice_in_dim(inv_pad, start, width, 0).reshape(REACH_MAX + 1, BLOCK)
        scaled = gram * inv_rows[None, :, None] * inv_cols[:, None, :]
        valid = offsets <= reach[block_index]
        return jnp.where(valid[:, None, None], scaled, jnp.float32(0.0))
    return lax.map(one_block, jnp.arange(nblocks, dtype=jnp.int32))
```

```python
import functools

import jax
import jax.numpy as jnp
from jax import lax
from jax.experimental import pallas as pl
from jax.experimental.pallas import tpu as pltpu
from jax.sharding import PartitionSpec as P

BLOCK = 512
REACH_MAX = 6
QUARTER = 128
HALF = 64
TAIL = 16
FULL = 32766.0
VMEM = pl.BlockSpec(memory_space=pltpu.VMEM)
SMEM = pl.BlockSpec(memory_space=pltpu.SMEM)


def call(kernel, out_shape, smem, *operands):
    size = lambda a: a.size * a.dtype.itemsize
    moved = sum(size(a) for a in operands) + sum(size(a) for a in out_shape)
    return pl.pallas_call(
        kernel,
        out_shape=out_shape,
        in_specs=[SMEM] * len(smem) + [VMEM] * len(operands),
        out_specs=[VMEM] * len(out_shape),
        compiler_params=pltpu.CompilerParams(vmem_limit_bytes=32 << 20),
        cost_estimate=pl.CostEstimate(flops=moved, bytes_accessed=moved, transcendentals=0),
    )(*smem, *operands)


def exponent_of(most):
    return jnp.clip(jnp.ceil(jnp.log2(jnp.maximum(most, 1e-30))), -100.0, 100.0)


def encode(value, exponent):
    part = jnp.abs(value) * jnp.exp2(-exponent)
    root = jnp.sqrt(jnp.maximum(part, 1e-30)) * FULL
    root = jnp.minimum(root, FULL)
    return jnp.round(jnp.where(value < 0, -root, root)).astype(jnp.int32).astype(jnp.int16)


def decode(code, exponent):
    root = code.astype(jnp.int32).astype(jnp.float32)
    return root * jnp.abs(root) * (jnp.exp2(exponent) * (1.0 / (FULL * FULL)))


def put_exponent(message, rows, tile, exponent):
    message[rows : rows + TAIL, tile * 128 : tile * 128 + 128] = (
        jnp.broadcast_to(exponent, (TAIL, 128)).astype(jnp.int32).astype(jnp.int16)
    )


def get_exponent(message, rows, tile):
    held = message[rows : rows + TAIL, tile * 128 : tile * 128 + 128]
    return jnp.max(held.astype(jnp.int32).astype(jnp.float32), axis=(0, 1), keepdims=True)


def pack_kernel(tiles, place, *refs):
    count = len(tiles)
    sums, (own, right, left, keep) = refs[:-4], refs[-4:]
    x = place[0]

    def quarter(steps, half):
        return pl.multiple_of(lax.rem(x + steps, 4) * QUARTER + half * HALF, HALF)

    for t, (ref, row, col) in enumerate(tiles):
        src = sums[ref]
        cols = slice(col, col + BLOCK)

        def most_of(i, most):
            rows = pl.ds(pl.multiple_of(row + i * HALF, HALF), HALF)
            return jnp.maximum(most, jnp.abs(src[rows, cols]))

        most = lax.fori_loop(0, BLOCK // HALF, most_of, jnp.zeros((HALF, BLOCK), jnp.float32))
        exponent = exponent_of(jnp.max(most, axis=(0, 1), keepdims=True))

        def rows_of(steps, half):
            return src[pl.ds(row + quarter(steps, half), HALF), cols]

        base = t * QUARTER
        for half in range(2):
            own[t, half * HALF : (half + 1) * HALF, :] = rows_of(0, half)
        right[base : base + HALF, :] = encode(rows_of(2, 0), exponent)
        right[base + HALF : base + QUARTER, :] = encode(rows_of(1, 1), exponent)
        left[base : base + HALF, :] = encode(rows_of(2, 1), exponent)
        left[base + HALF : base + QUARTER, :] = encode(rows_of(3, 0), exponent)
        keep[t, 0:HALF, :] = rows_of(1, 0)
        keep[t, HALF:QUARTER, :] = rows_of(3, 1)
        put_exponent(right, count * QUARTER, t, exponent)
        put_exponent(left, count * QUARTER, t, exponent)


def pass_kernel(count, own, keep, from_left, from_right, total, right, left):
    for t in range(count):
        base = t * QUARTER
        left_exp = get_exponent(from_left, count * QUARTER, t)
        right_exp = get_exponent(from_right, count * QUARTER, t)
        total[t, HALF:QUARTER, :] = own[t, HALF:QUARTER, :] + decode(
            from_left[base + HALF : base + QUARTER, :], left_exp
        )
        total[t, 0:HALF, :] = own[t, 0:HALF, :] + decode(
            from_right[base + HALF : base + QUARTER, :], right_exp
        )
        to_right = keep[t, 0:HALF, :] + decode(from_left[base : base + HALF, :], left_exp)
        to_left = keep[t, HALF:QUARTER, :] + decode(from_right[base : base + HALF, :], right_exp)
        for message, value in ((right, to_right), (left, to_left)):
            exponent = exponent_of(jnp.max(jnp.abs(value), axis=(0, 1), keepdims=True))
            message[t * HALF : (t + 1) * HALF, :] = encode(value, exponent)
            put_exponent(message, count * HALF, t, exponent)


def sum_kernel(count, total, from_left, from_right, out):
    for t in range(count):
        rows = slice(t * HALF, (t + 1) * HALF)
        out[t, 0:HALF, :] = total[t, 0:HALF, :] + decode(
            from_left[rows, :], get_exponent(from_left, count * HALF, t)
        )
        out[t, HALF:QUARTER, :] = total[t, HALF:QUARTER, :] + decode(
            from_right[rows, :], get_exponent(from_right, count * HALF, t)
        )


def finish_kernel(place, reach, rows, cols, s0, s0b, s1, s2, s3, z1, z2, z3, swapped, out):
    core = place[1]

    def write(block, offset, value):
        inside = (offset <= reach[block]).astype(jnp.float32)
        scaled = (value * rows[block * QUARTER : (block + 1) * QUARTER, :]) * cols[
            block + offset : block + offset + 1, :
        ]
        out[block, offset] = jnp.where(inside > 0, scaled, 0.0)

    write(0, 0, s0[0])
    write(0, 1, s0[1])
    write(1, 0, s0[2])

    @pl.when(core == 0)
    def _():
        write(0, 2, s0b[0])
        write(0, 3, s0b[1])
        for k, held in ((1, s1), (2, s2), (3, s3)):
            write(0, 3 + k, held[0])
            write(1, 2 + k, held[1])
        write(1, 1, swapped[0])
        write(1, 2, swapped[1])
        write(1, 6, z3[0])

    @pl.when(core == 1)
    def _():
        for k, held in ((1, s1), (2, s2), (3, s3)):
            write(0, 1 + k, held[0])
            write(1, k, held[1])
        write(1, 4, swapped[0])
        write(0, 5, swapped[1])
        write(1, 5, z1[0])
        write(1, 6, z2[0])
        write(0, 6, z3[0])


def dot_t(a, b):
    return lax.dot_general(a, b, (((1,), (1,)), ((), ())), preferred_element_type=jnp.float32)


def per_device(dosages, reach, counts):
    snp_size = lax.axis_size("snp")
    chips = snp_size // 2
    snp = lax.axis_index("snp")
    x = lax.axis_index("smp")
    core = lax.rem(snp, 2)
    first_core = core == 0
    place = jnp.stack([x, core]).astype(jnp.int32)
    ring = range(4)

    def to_right(v):
        return lax.ppermute(v, "smp", [(i, (i + 1) % 4) for i in ring])

    def to_left(v):
        return lax.ppermute(v, "smp", [(i, (i + 3) % 4) for i in ring])

    def swap(v):
        return lax.ppermute(v, "snp", [(i, i ^ 1) for i in range(snp_size)])

    def halo(v, low, high):
        pairs = []
        for chip in range(chips):
            for kind, by in ((0, low), (1, high)):
                if 0 <= chip + by < chips:
                    pairs.append((2 * chip + kind, 2 * (chip + by) + kind))
        return lax.ppermute(v, "snp", pairs)

    def home(v):
        pairs = [(2 * c + k, 2 * (c - 1) + 1 - k) for c in range(1, chips) for k in range(2)]
        return lax.ppermute(v, "snp", pairs)

    def block(number):
        return lax.dynamic_slice_in_dim(dosages, number * BLOCK, BLOCK, 0)

    def pick(a, b):
        return jnp.where(first_core, a, b)

    near = block(core)
    far = block(1 - core)
    h1 = halo(near, -1, 1)
    other = swap(dosages)
    h2 = halo(far, -1, 1)
    h3 = halo(far, 1, -1)
    g1, g2, g3 = swap(h1), swap(h2), swap(h3)
    o0, o1 = dosages[:BLOCK], dosages[BLOCK:]

    def reduce_tiles(tiles, sums):
        count = len(tiles)
        f32 = jax.ShapeDtypeStruct((count, QUARTER, BLOCK), jnp.float32)
        s16 = lambda rows: jax.ShapeDtypeStruct((count * rows + TAIL, BLOCK), jnp.int16)
        own, right, left, keep = call(
            functools.partial(pack_kernel, tiles), [f32, s16(QUARTER), s16(QUARTER), f32], [place], *sums
        )
        from_left, from_right = to_right(right), to_left(left)
        total, right, left = call(
            functools.partial(pass_kernel, count), [f32, s16(HALF), s16(HALF)], [], own, keep, from_left, from_right
        )
        from_left, from_right = to_right(right), to_left(left)
        return call(functools.partial(sum_kernel, count), [f32], [], total, from_left, from_right)[0]

    column = ((0, 0, 0), (0, BLOCK, 0), (1, 0, 0))
    s0 = reduce_tiles(((0, 0, 0), (0, 0, BLOCK), (1, 0, 0)), [dot_t(o0, dosages), dot_t(o1, o1)])
    s0b = reduce_tiles(
        ((0, 0, 0), (0, 0, BLOCK)), [dot_t(pick(o0, other[BLOCK:]), pick(other, dosages))]
    )
    n1, n2, n3 = pick(h1, g1), pick(h2, g2), pick(g3, h3)
    s1 = reduce_tiles(column, [dot_t(dosages, n1), dot_t(pick(g1, h1), pick(n1, o1))])
    s2 = reduce_tiles(column, [dot_t(dosages, n2), dot_t(pick(g1, h2), pick(n2, o1))])
    s3 = reduce_tiles(column, [dot_t(dosages, n3), dot_t(pick(g2, g3), pick(n1, o1))])
    z1, z2, z3 = home(s1[2:3]), home(s2[2:3]), home(s3[2:3])
    swapped = swap(pick(jnp.concatenate([z1, z2]), s0b))

    inv = lax.rsqrt(counts.astype(jnp.float32))
    inv = jnp.concatenate([inv, jnp.ones((REACH_MAX * BLOCK,), jnp.float32)])
    cols = lax.dynamic_slice_in_dim(inv, snp * 2 * BLOCK, 8 * BLOCK, 0).reshape(8, BLOCK)
    rows = lax.dynamic_slice_in_dim(cols[:2], x * QUARTER, QUARTER, 1).reshape(2 * QUARTER, 1)
    here = lax.dynamic_slice_in_dim(reach, snp * 2, 2, 0)

    def finish(place, here, *operands):
        return call(
            finish_kernel,
            [jax.ShapeDtypeStruct((2, REACH_MAX + 1, QUARTER, BLOCK), jnp.float32)],
            [place, here],
            *operands,
        )[0]

    return finish(place, here, rows, cols, s0, s0b, s1, s2, s3, z1, z2, z3, swapped)


def solution(mesh):
    in_specs = (P("snp", "smp"), P(), P())
    out_specs = P("snp", None, "smp", None)
    return jax.shard_map(
        per_device, mesh=mesh, in_specs=in_specs, out_specs=out_specs, check_vma=False
    )
```

```python
import functools

import jax
import jax.numpy as jnp
from jax import lax
from jax.experimental import pallas as pl
from jax.experimental.pallas import tpu as pltpu
from jax.sharding import PartitionSpec as P

BLOCK = 512
REACH_MAX = 6
QUARTER = 128
HALF = 64
TAIL = 16
CUT = 256
FULL = 32766.0
VMEM = pl.BlockSpec(memory_space=pltpu.VMEM)
SMEM = pl.BlockSpec(memory_space=pltpu.SMEM)
ANY = pl.BlockSpec(memory_space=pl.ANY)
F32 = jnp.float32
STAGES = {"a": 3, "b": 4, "c": 4, "d": 2, "e": 2}


def exponent_of(most):
    return jnp.clip(jnp.ceil(jnp.log2(jnp.maximum(most, 1e-30))), -100.0, 100.0)


def encode(value, exponent):
    part = jnp.abs(value) * jnp.exp2(-exponent)
    root = jnp.sqrt(jnp.maximum(part, 1e-30)) * FULL
    root = jnp.minimum(root, FULL)
    return jnp.round(jnp.where(value < 0, -root, root)).astype(jnp.int32).astype(jnp.int16)


def decode(code, exponent):
    root = code.astype(jnp.int32).astype(F32)
    return root * jnp.abs(root) * (jnp.exp2(exponent) * (1.0 / (FULL * FULL)))


def put_exponent(message, row, tile, exponent):
    message[row : row + TAIL, tile * 128 : tile * 128 + 128] = (
        jnp.broadcast_to(exponent, (TAIL, 128)).astype(jnp.int32).astype(jnp.int16)
    )


def get_exponent(message, row, tile):
    held = message[row : row + TAIL, tile * 128 : tile * 128 + 128]
    return jnp.max(held.astype(jnp.int32).astype(F32), axis=(0, 1), keepdims=True)


def section_rows(section):
    part, stage = section
    return STAGES[stage] * (QUARTER if part == 1 else HALF)


def layout(sections):
    first, places = 0, {}
    for section in sections:
        places[section] = first
        first += section_rows(section)
    return {s: (at, first + TAIL * n) for n, (s, at) in enumerate(places.items())}, first + TAIL * len(sections)


def pack(stage, x, acc, right, left, at, own, keep):
    def quarter(steps, half):
        return pl.multiple_of(lax.rem(x + steps, 4) * QUARTER + half * HALF, HALF)

    for t in range(STAGES[stage]):

        def most_of(i, most):
            return jnp.maximum(most, jnp.abs(acc[t, pl.ds(pl.multiple_of(i * HALF, HALF), HALF), :]))

        most = lax.fori_loop(0, BLOCK // HALF, most_of, jnp.zeros((HALF, BLOCK), F32))
        exponent = exponent_of(jnp.max(most, axis=(0, 1), keepdims=True))

        def rows_of(steps, half):
            return acc[t, pl.ds(quarter(steps, half), HALF), :]

        base = at[0] + t * QUARTER
        for half in range(2):
            own[t, half * HALF : (half + 1) * HALF, :] = rows_of(0, half)
        right[base : base + HALF, :] = encode(rows_of(2, 0), exponent)
        right[base + HALF : base + QUARTER, :] = encode(rows_of(1, 1), exponent)
        left[base : base + HALF, :] = encode(rows_of(2, 1), exponent)
        left[base + HALF : base + QUARTER, :] = encode(rows_of(3, 0), exponent)
        keep[t, 0:HALF, :] = rows_of(1, 0)
        keep[t, HALF:QUARTER, :] = rows_of(3, 1)
        put_exponent(right, at[1], t, exponent)
        put_exponent(left, at[1], t, exponent)


def pass_on(stage, own, keep, come, come_at, total, right, left, at):
    from_left, from_right = come
    for t in range(STAGES[stage]):
        base = come_at[0] + t * QUARTER
        left_exp = get_exponent(from_left, come_at[1], t)
        right_exp = get_exponent(from_right, come_at[1], t)
        total[t, HALF:QUARTER, :] = own[t, HALF:QUARTER, :] + decode(
            from_left[base + HALF : base + QUARTER, :], left_exp
        )
        total[t, 0:HALF, :] = own[t, 0:HALF, :] + decode(
            from_right[base + HALF : base + QUARTER, :], right_exp
        )
        to_right = keep[t, 0:HALF, :] + decode(from_left[base : base + HALF, :], left_exp)
        to_left = keep[t, HALF:QUARTER, :] + decode(from_right[base : base + HALF, :], right_exp)
        first = at[0] + t * HALF
        for message, value in ((right, to_right), (left, to_left)):
            exponent = exponent_of(jnp.max(jnp.abs(value), axis=(0, 1), keepdims=True))
            message[first : first + HALF, :] = encode(value, exponent)
            put_exponent(message, at[1], t, exponent)


def add_up(stage, total, come, come_at, out):
    from_left, from_right = come
    for t in range(STAGES[stage]):
        first = come_at[0] + t * HALF
        out[t, 0:HALF, :] = total[t, 0:HALF, :] + decode(
            from_left[first : first + HALF, :], get_exponent(from_left, come_at[1], t)
        )
        out[t, HALF:QUARTER, :] = total[t, HALF:QUARTER, :] + decode(
            from_right[first : first + HALF, :], get_exponent(from_right, come_at[1], t)
        )


def dot_t(a, b):
    return lax.dot_general(a, b, (((1,), (1,)), ((), ())), preferred_element_type=F32)


def tile(acc, t, rows, row, cols, col):
    @pl.loop(0, BLOCK // CUT)
    def _(i):
        at = pl.multiple_of(i * CUT, CUT)
        acc[t, pl.ds(at, CUT), :] = dot_t(
            rows[pl.ds(row + at, CUT), :], cols[col : col + BLOCK, :]
        )


def narrow(acc, t, col, rows, row, cols):
    @pl.loop(0, BLOCK // CUT)
    def _(i):
        at = pl.multiple_of(i * CUT, CUT)
        acc[t, pl.ds(at, CUT), col : col + CUT] = dot_t(rows[pl.ds(row + at, CUT), :], cols[...])


class Reduction:
    def __init__(self, place):
        self.place = place
        self.held, self.come, self.sums = {}, {}, {}
        self.token = jnp.zeros((8, 128), F32)

    def step(self, work=None, operands=(), pack_of=None, passes=(), sums=(), sections=(), copies=(), sends=(), flops=0):
        arrays, places = [], {}

        def take(key, value):
            if key not in places:
                places[key] = len(arrays)
                arrays.append(value)

        for n, operand in enumerate(operands):
            take(("operand", n), operand)
        for stage in passes:
            take(("own", stage), self.held["own", stage])
            take(("keep", stage), self.held["keep", stage])
        for stage in sums:
            take(("total", stage), self.held["total", stage])
        take(("token",), self.token)
        come = dict(self.come)
        for source in [(1, s) for s in passes] + [(2, s) for s in sums]:
            number, pair, _ = come[source]
            take(("come", number, 0), pair[0])
            take(("come", number, 1), pair[1])
        outs, shapes = {}, []

        def give(key, shape, dtype=F32):
            outs[key] = len(shapes)
            shapes.append(jax.ShapeDtypeStruct(shape, dtype))

        give(("token",), (8, 128))
        at, rows = layout(sections)
        if sections:
            give("right", (rows, BLOCK), jnp.int16)
            give("left", (rows, BLOCK), jnp.int16)
        if pack_of:
            give(("own", pack_of), (STAGES[pack_of], QUARTER, BLOCK))
            give(("keep", pack_of), (STAGES[pack_of], QUARTER, BLOCK))
        for stage in passes:
            give(("total", stage), (STAGES[stage], QUARTER, BLOCK))
        for stage in sums:
            give(("sum", stage), (STAGES[stage], QUARTER, BLOCK))
        for n, (coded, *tiles) in enumerate(sends):
            if coded:
                give(("send", n), (len(tiles) * QUARTER + TAIL, BLOCK), jnp.int16)
            else:
                give(("send", n), (len(tiles), QUARTER, BLOCK))
        for n, (count, operand, _) in enumerate(copies):
            give(("copy", n), (count, operands[operand].shape[1]), operands[operand].dtype)

        def kernel(place, *refs):
            ins, made = refs[: len(arrays)], refs[len(arrays) : len(arrays) + len(shapes)]
            acc, sems = refs[-2:]
            x, core = place[0], place[1]
            made[0][...] = ins[places[("token",)]][...]
            get = lambda *key: ins[places[key]]
            out = lambda *key: made[outs[key if len(key) > 1 else key[0]]]
            moves = []
            for n, (count, operand, first) in enumerate(copies):
                source = ins[operand].at[pl.ds(pl.multiple_of(first(core), CUT), count), :]
                moves.append(pltpu.make_async_copy(source, out("copy", n), sems.at[n]))
                moves[-1].start()
            if work is not None:
                work(core, ins[: len(operands)], acc)
            if pack_of:
                pack(pack_of, x, acc, out("right"), out("left"), at[1, pack_of], out("own", pack_of), out("keep", pack_of))
            for stage in passes:
                number, _, where = come[1, stage]
                pass_on(
                    stage, get("own", stage), get("keep", stage), (get("come", number, 0), get("come", number, 1)), where,
                    out("total", stage), out("right"), out("left"), at[2, stage],
                )
            for stage in sums:
                number, _, where = come[2, stage]
                add_up(stage, get("total", stage), (get("come", number, 0), get("come", number, 1)), where, out("sum", stage))
            for n, (coded, *tiles) in enumerate(sends):
                for i, (first, second) in enumerate(tiles):
                    value = out("sum", first[0])[first[1]]
                    if first != second:
                        value = jnp.where(core == 0, value, out("sum", second[0])[second[1]])
                    if coded:
                        exponent = exponent_of(jnp.max(jnp.abs(value), axis=(0, 1), keepdims=True))
                        out("send", n)[i * QUARTER : (i + 1) * QUARTER, :] = encode(value, exponent)
                        put_exponent(out("send", n), len(tiles) * QUARTER, i, exponent)
                    else:
                        out("send", n)[i] = value
            for move in moves:
                move.wait()

        size = lambda a: a.size * a.dtype.itemsize
        depth = STAGES[pack_of] if pack_of else 1
        made = pl.pallas_call(
            kernel,
            out_shape=shapes,
            in_specs=[SMEM] + [VMEM] * len(arrays),
            out_specs=[VMEM] * len(shapes),
            scratch_shapes=[pltpu.VMEM((depth, BLOCK, BLOCK), F32), pltpu.SemaphoreType.DMA((max(1, len(copies)),))],
            compiler_params=pltpu.CompilerParams(vmem_limit_bytes=16 << 20),
            cost_estimate=pl.CostEstimate(
                flops=10**11, bytes_accessed=0, transcendentals=0
            ),
        )(self.place, *arrays)
        self.token = made[0]
        for key, n in outs.items():
            if key[0] in ("own", "keep", "total"):
                self.held[key] = made[n]
            if key[0] == "sum":
                self.sums[key[1]] = made[n]
        if sections:
            pair = tuple(
                lax.ppermute(made[outs[side]], "smp", [(i, (i + by) % 4) for i in range(4)])
                for side, by in (("right", 1), ("left", 3))
            )
            number = len(self.come)
            for section in sections:
                self.come[section] = (number, pair, at[section])
        return [made[n] for key, n in outs.items() if key[0] in ("copy", "send")]


def decoded(coded, count, tile):
    return decode(coded[tile * QUARTER : (tile + 1) * QUARTER, :], get_exponent(coded, count * QUARTER, tile))


def scaled(value, reach, rows, cols, block, offset, cut=slice(0, BLOCK)):
    inside = (offset <= reach[block]).astype(F32)
    product = (value * rows[block * QUARTER : (block + 1) * QUARTER, :]) * cols[
        block + offset : block + offset + 1, cut
    ]
    return jnp.where(inside > 0, product, 0.0)


def own_work(core, refs, acc):
    (d,) = refs
    tile(acc, 0, d, 0, d, 0)
    tile(acc, 1, d, 0, d, BLOCK)
    tile(acc, 2, d, BLOCK, d, BLOCK)


def four_rows(d, other):
    return enumerate(((d, 0), (d, BLOCK), (other, 0), (other, BLOCK)))


def b_work(core, refs, acc):
    d, other, h1 = refs

    @pl.when(core == 0)
    def _():
        for t, (rows, row) in four_rows(d, other):
            tile(acc, t, rows, row, h1, 0)

    @pl.when(core == 1)
    def _():
        for t in range(4):
            tile(acc, t, other, (t // 2) * BLOCK, d, (t % 2) * BLOCK)


def c_work(core, refs, acc):
    d, other, h1, h2, m1 = refs[:5]

    @pl.when(core == 0)
    def _():
        for t, (rows, row) in four_rows(d, other):
            tile(acc, t, rows, row, h2, 0)

    @pl.when(core == 1)
    def _():
        tile(acc, 0, h1, 0, d, BLOCK)
        tile(acc, 1, h2, 0, d, BLOCK)
        tile(acc, 2, h1, 0, m1, 0)
        tile(acc, 3, h2, 0, m1, 0)


def d_work(core, refs, acc):
    d, other, h3 = refs

    @pl.when(core == 0)
    def _():
        for t, (rows, row) in four_rows(d, other):
            narrow(acc, t // 2, (t % 2) * CUT, rows, row, h3)

    @pl.when(core == 1)
    def _():
        acc[...] = jnp.zeros_like(acc)


def e_work(core, refs, acc):
    d, other, h1, h3, h4, m2 = refs

    @pl.when(core == 0)
    def _():
        for t, (rows, row) in four_rows(d, other):
            narrow(acc, t // 2, (t % 2) * CUT, rows, row, h4)

    @pl.when(core == 1)
    def _():
        acc[0, 0:CUT, :] = dot_t(h3[...], d[BLOCK : 2 * BLOCK, :])
        acc[0, CUT:BLOCK, :] = dot_t(h4[...], d[BLOCK : 2 * BLOCK, :])
        tile(acc, 1, h1, 0, m2, 0)


def near_kernel(place, d, near, sem):
    copies = []
    for n in range(8):
        first = n * HALF
        source = d.at[pl.ds(pl.multiple_of(place[1] * BLOCK + first, HALF), HALF), :]
        copies.append(pltpu.make_async_copy(source, near.at[first : first + HALF, :], sem.at[n]))
        copies[-1].start()
    for copy in copies:
        copy.wait()


def most_kernel(place, reach, rows, cols, a, b, c, swapped, zc, out):
    core = place[1]

    def write(block, offset, value):
        out[block, offset] = scaled(value, reach, rows, cols, block, offset)

    write(0, 0, a[0])
    write(0, 1, a[1])
    write(1, 0, a[2])

    @pl.when(core == 0)
    def _():
        write(0, 2, swapped[0])
        write(0, 3, swapped[1])
        write(1, 1, swapped[2])
        write(1, 2, swapped[3])
        write(0, 4, b[0])
        write(1, 3, b[1])
        write(0, 5, c[0])
        write(1, 4, c[1])

    @pl.when(core == 1)
    def _():
        write(0, 2, swapped[0])
        write(1, 1, swapped[1])
        write(0, 3, swapped[2])
        write(1, 2, swapped[3])
        write(1, 4, decoded(zc, 4, 0))
        write(0, 5, decoded(zc, 4, 1))
        write(1, 5, decoded(zc, 4, 2))
        write(0, 6, decoded(zc, 4, 3))


def last_kernel(place, reach, rows, cols, d, e, crossed, edge, held, out, room, sem):
    del held
    core = place[1]
    sides = ((slice(0, CUT), 0), (slice(CUT, BLOCK), 1))

    def put(slot, block, offset, value, cut):
        room[slot, :, cut] = scaled(value, reach, rows, cols, block, offset, cut)

    def send(slot, block, offset):
        copy = pltpu.make_async_copy(room.at[slot], out.at[block, offset], sem.at[slot])
        copy.start()
        return copy

    @pl.when(core == 0)
    def _():
        copies = []
        for block, (at, _) in enumerate(sides):
            for (cut, _), held in zip(sides, (d, e)):
                put(block, block, 6 - block, held[0, :, at], cut)
            copies.append(send(block, block, 6 - block))
        put(2, 1, 6, decoded(crossed, 2, 0), slice(0, BLOCK))
        copies.append(send(2, 1, 6))
        for copy in copies:
            copy.wait()

    @pl.when(core == 1)
    def _():
        copies = []
        halves = [decoded(crossed, 2, side) for side in range(2)]
        for block, (at, _) in enumerate(sides):
            for cut, side in sides:
                put(block, block, 4 - block, halves[side][:, at], cut)
            copies.append(send(block, block, 4 - block))
        put(2, 1, 6, decoded(edge, 1, 0), slice(0, BLOCK))
        copies.append(send(2, 1, 6))
        for copy in copies:
            copy.wait()


def per_device(dosages, reach, counts):
    snp_size = lax.axis_size("snp")
    chips = snp_size // 2
    snp = lax.axis_index("snp")
    x = lax.axis_index("smp")
    core = lax.rem(snp, 2)
    place = jnp.stack([x, core]).astype(jnp.int32)

    def hop(v, *moves):
        pairs = [
            (2 * chip + source, 2 * (chip + by) + target)
            for chip in range(chips)
            for source, by, target in moves
            if 0 <= chip + by < chips
        ]
        return lax.ppermute(v, "snp", pairs)

    flops = lambda tiles: 2 * tiles * BLOCK * BLOCK * dosages.shape[1]
    net = Reduction(place)
    far = lambda more: lambda core: (1 - core) * BLOCK + more
    whole = lambda core: 0
    block_shape = jax.ShapeDtypeStruct((BLOCK, dosages.shape[1]), dosages.dtype)

    near = pl.pallas_call(
        near_kernel,
        out_shape=block_shape,
        in_specs=[SMEM, ANY],
        out_specs=VMEM,
        scratch_shapes=[pltpu.SemaphoreType.DMA((8,))],
    )(place, dosages)
    h1 = hop(near, (0, -1, 0), (1, 1, 1))
    other = hop(dosages, (0, 0, 1), (1, 0, 0))
    (far2,) = net.step(
        own_work, [dosages], "a", sections=[(1, "a")], copies=[(BLOCK, 0, far(0))], flops=flops(3)
    )
    h2 = hop(far2, (0, -1, 0), (1, 1, 1))
    m1 = hop(h1, (0, 0, 1))
    (far3,) = net.step(
        b_work, [dosages, other, h1], "b", passes=["a"], sections=[(1, "b"), (2, "a")],
        copies=[(CUT, 0, far(0))], flops=flops(4),
    )
    h3 = hop(far3, (1, -1, 0), (0, 1, 1))
    inv = lax.rsqrt(counts.astype(F32))
    inv = jnp.concatenate([inv, jnp.ones((REACH_MAX * BLOCK,), F32)])
    cols = lax.dynamic_slice_in_dim(inv, snp * 2 * BLOCK, 8 * BLOCK, 0).reshape(8, BLOCK)
    rows = lax.dynamic_slice_in_dim(cols[:2], x * QUARTER, QUARTER, 1).reshape(2 * QUARTER, 1)
    here = lax.dynamic_slice_in_dim(reach, snp * 2, 2, 0)
    far4, forward = net.step(
        c_work, [dosages, other, h1, h2, m1, rows, cols], "c", sections=[(1, "c")],
        copies=[(CUT, 0, far(CUT)), (BLOCK, 3, whole)], flops=flops(4),
    )
    h4 = hop(far4, (1, -1, 0), (0, 1, 1))
    m2 = hop(forward, (0, 0, 1))
    net.step(
        d_work, [dosages, other, h3], "d", passes=["b"], sums=["a"], sections=[(1, "d"), (2, "b")], flops=flops(2)
    )
    net.step(
        e_work, [dosages, other, h1, h3, h4, m2], "e", passes=["c"], sections=[(1, "e"), (2, "c")], flops=flops(2)
    )
    swapping, coded_c = net.step(
        passes=["d", "e"], sums=["b", "c"], sections=[(2, "d"), (2, "e")],
        sends=[
            (False, (("b", 2), ("b", 0)), (("b", 3), ("b", 1)), (("c", 2), ("b", 2)), (("c", 3), ("b", 3))),
            (True, *(((stage, t),) * 2 for stage, t in (("c", 0), ("c", 1), ("c", 2), ("c", 3)))),
        ],
    )
    swapped = hop(swapping, (0, 0, 1), (1, 0, 0))
    zc = hop(coded_c, (1, -1, 1))
    crossing, ending = net.step(
        sums=["d", "e"],
        sends=[(True, (("d", 1), ("e", 0)), (("e", 1), ("e", 1))), (True, (("e", 1), ("e", 1)))],
    )
    crossed = hop(crossing, (0, 0, 1), (1, -1, 0))
    edge = hop(ending, (1, -1, 1))
    out_shape = jax.ShapeDtypeStruct((2, REACH_MAX + 1, QUARTER, BLOCK), F32)
    s = net.sums
    parts = (rows, cols, s["a"], s["b"], s["c"], swapped, zc)
    out = pl.pallas_call(
        most_kernel,
        out_shape=out_shape,
        in_specs=[SMEM] * 2 + [VMEM] * len(parts),
        out_specs=VMEM,
        compiler_params=pltpu.CompilerParams(vmem_limit_bytes=16 << 20),
        cost_estimate=pl.CostEstimate(flops=10**11, bytes_accessed=0, transcendentals=0),
    )(place, here, *parts)
    return pl.pallas_call(
        last_kernel,
        out_shape=out_shape,
        in_specs=[SMEM] * 2 + [VMEM] * 6 + [ANY],
        out_specs=ANY,
        scratch_shapes=[pltpu.VMEM((3, QUARTER, BLOCK), F32), pltpu.SemaphoreType.DMA((3,))],
        input_output_aliases={8: 0},
        compiler_params=pltpu.CompilerParams(vmem_limit_bytes=8 << 20),
    )(place, here, rows, cols, s["d"], s["e"], crossed, edge, out)


def solution(mesh):
    in_specs = (P("snp", "smp"), P(), P())
    out_specs = P("snp", None, "smp", None)
    return jax.shard_map(
        per_device, mesh=mesh, in_specs=in_specs, out_specs=out_specs, check_vma=False
    )
```

```python
import functools

import jax
import jax.numpy as jnp
from jax import lax
from jax.experimental import pallas as pl
from jax.experimental.pallas import tpu as pltpu
from jax.sharding import PartitionSpec as P

BLOCK = 512
REACH_MAX = 6
QUARTER = 128
HALF = 64
TAIL = 16
CUT = 256
FULL = 32766.0
VMEM = pl.BlockSpec(memory_space=pltpu.VMEM)
SMEM = pl.BlockSpec(memory_space=pltpu.SMEM)
ANY = pl.BlockSpec(memory_space=pl.ANY)
F32 = jnp.float32
STAGES = {"a": 3, "b": 4, "c": 4, "d": 2, "e": 2}


def exponent_of(most):
    return jnp.clip(jnp.ceil(jnp.log2(jnp.maximum(most, 1e-30))), -100.0, 100.0)


def encode(value, exponent):
    part = jnp.maximum(jnp.abs(value) * (jnp.exp2(-exponent) * (FULL * FULL)), 1e-20)
    root = jnp.minimum(part * lax.rsqrt(part), FULL)
    root = (root + 0.5).astype(jnp.int32)
    return jnp.where(value < 0, -root, root).astype(jnp.int16)


def decode(code, exponent):
    root = code.astype(jnp.int32).astype(F32)
    return root * jnp.abs(root) * (jnp.exp2(exponent) * (1.0 / (FULL * FULL)))


def put_exponent(message, row, tile, exponent):
    message[row : row + TAIL, tile * 128 : tile * 128 + 128] = (
        jnp.broadcast_to(exponent, (TAIL, 128)).astype(jnp.int32).astype(jnp.int16)
    )


def get_exponent(message, row, tile):
    held = message[row : row + TAIL, tile * 128 : tile * 128 + 128]
    return jnp.max(held.astype(jnp.int32).astype(F32), axis=(0, 1), keepdims=True)


def section_rows(section):
    part, stage = section
    return STAGES[stage] * (QUARTER if part == 1 else HALF)


def layout(sections):
    first, places = 0, {}
    for section in sections:
        places[section] = first
        first += section_rows(section)
    return {s: (at, first + TAIL * n) for n, (s, at) in enumerate(places.items())}, first + TAIL * len(sections)


def pack(stage, x, acc, right, left, at, own, keep):
    def quarter(steps, half):
        return pl.multiple_of(lax.rem(x + steps, 4) * QUARTER + half * HALF, HALF)

    for t in range(STAGES[stage]):
        most = jnp.zeros((TAIL, BLOCK), F32)
        for first in range(0, BLOCK, TAIL):
            most = jnp.maximum(most, jnp.abs(acc[t, first : first + TAIL, :]))
        exponent = exponent_of(jnp.max(most, axis=(0, 1), keepdims=True))

        def rows_of(steps, half):
            return acc[t, pl.ds(quarter(steps, half), HALF), :]

        base = at[0] + t * QUARTER
        for half in range(2):
            own[t, half * HALF : (half + 1) * HALF, :] = rows_of(0, half)
        right[base : base + HALF, :] = encode(rows_of(2, 0), exponent)
        right[base + HALF : base + QUARTER, :] = encode(rows_of(1, 1), exponent)
        left[base : base + HALF, :] = encode(rows_of(2, 1), exponent)
        left[base + HALF : base + QUARTER, :] = encode(rows_of(3, 0), exponent)
        keep[t, 0:HALF, :] = rows_of(1, 0)
        keep[t, HALF:QUARTER, :] = rows_of(3, 1)
        put_exponent(right, at[1], t, exponent)
        put_exponent(left, at[1], t, exponent)


def pass_on(stage, own, keep, come, come_at, total, right, left, at):
    from_left, from_right = come
    for t in range(STAGES[stage]):
        base = come_at[0] + t * QUARTER
        left_exp = get_exponent(from_left, come_at[1], t)
        right_exp = get_exponent(from_right, come_at[1], t)
        total[t, HALF:QUARTER, :] = own[t, HALF:QUARTER, :] + decode(
            from_left[base + HALF : base + QUARTER, :], left_exp
        )
        total[t, 0:HALF, :] = own[t, 0:HALF, :] + decode(
            from_right[base + HALF : base + QUARTER, :], right_exp
        )
        to_right = keep[t, 0:HALF, :] + decode(from_left[base : base + HALF, :], left_exp)
        to_left = keep[t, HALF:QUARTER, :] + decode(from_right[base : base + HALF, :], right_exp)
        first = at[0] + t * HALF
        for message, value in ((right, to_right), (left, to_left)):
            exponent = exponent_of(jnp.max(jnp.abs(value), axis=(0, 1), keepdims=True))
            message[first : first + HALF, :] = encode(value, exponent)
            put_exponent(message, at[1], t, exponent)


def add_up(stage, total, come, come_at, out):
    from_left, from_right = come
    for t in range(STAGES[stage]):
        first = come_at[0] + t * HALF
        out[t, 0:HALF, :] = total[t, 0:HALF, :] + decode(
            from_left[first : first + HALF, :], get_exponent(from_left, come_at[1], t)
        )
        out[t, HALF:QUARTER, :] = total[t, HALF:QUARTER, :] + decode(
            from_right[first : first + HALF, :], get_exponent(from_right, come_at[1], t)
        )


def dot_t(a, b):
    return lax.dot_general(a, b, (((1,), (1,)), ((), ())), preferred_element_type=F32)


def tile(acc, t, rows, row, cols, col):
    acc[t] = dot_t(rows[row : row + BLOCK, :], cols[col : col + BLOCK, :])


def narrow(acc, t, col, rows, row, cols):
    acc[t, :, col : col + CUT] = dot_t(rows[row : row + BLOCK, :], cols[...])


class Reduction:
    def __init__(self, place):
        self.place = place
        self.held, self.come, self.sums = {}, {}, {}
        self.token = jnp.zeros((8, 128), F32)

    def step(self, work=None, operands=(), pack_of=None, passes=(), sums=(), sections=(), copies=(), sends=(), flops=0):
        arrays, places = [], {}

        def take(key, value):
            if key not in places:
                places[key] = len(arrays)
                arrays.append(value)

        for n, operand in enumerate(operands):
            take(("operand", n), operand)
        for stage in passes:
            take(("own", stage), self.held["own", stage])
            take(("keep", stage), self.held["keep", stage])
        for stage in sums:
            take(("total", stage), self.held["total", stage])
        take(("token",), self.token)
        come = dict(self.come)
        for source in [(1, s) for s in passes] + [(2, s) for s in sums]:
            number, pair, _ = come[source]
            take(("come", number, 0), pair[0])
            take(("come", number, 1), pair[1])
        outs, shapes = {}, []

        def give(key, shape, dtype=F32):
            outs[key] = len(shapes)
            shapes.append(jax.ShapeDtypeStruct(shape, dtype))

        give(("token",), (8, 128))
        at, rows = layout(sections)
        if sections:
            give("right", (rows, BLOCK), jnp.int16)
            give("left", (rows, BLOCK), jnp.int16)
        if pack_of:
            give(("own", pack_of), (STAGES[pack_of], QUARTER, BLOCK))
            give(("keep", pack_of), (STAGES[pack_of], QUARTER, BLOCK))
        for stage in passes:
            give(("total", stage), (STAGES[stage], QUARTER, BLOCK))
        for stage in sums:
            give(("sum", stage), (STAGES[stage], QUARTER, BLOCK))
        for n, (coded, *tiles) in enumerate(sends):
            if coded:
                give(("send", n), (len(tiles) * QUARTER + TAIL, BLOCK), jnp.int16)
            else:
                give(("send", n), (len(tiles), QUARTER, BLOCK))
        for n, (count, operand, _) in enumerate(copies):
            give(("copy", n), (count, operands[operand].shape[1]), operands[operand].dtype)

        def kernel(place, *refs):
            ins, made = refs[: len(arrays)], refs[len(arrays) : len(arrays) + len(shapes)]
            acc, sems = refs[-2:]
            x, core = place[0], place[1]
            made[0][...] = ins[places[("token",)]][...]
            get = lambda *key: ins[places[key]]
            out = lambda *key: made[outs[key if len(key) > 1 else key[0]]]
            moves = []
            for n, (count, operand, first) in enumerate(copies):
                source = ins[operand].at[pl.ds(pl.multiple_of(first(core), CUT), count), :]
                moves.append(pltpu.make_async_copy(source, out("copy", n), sems.at[n]))
                moves[-1].start()
            if work is not None:
                work(core, ins[: len(operands)], acc)
            if pack_of:
                pack(pack_of, x, acc, out("right"), out("left"), at[1, pack_of], out("own", pack_of), out("keep", pack_of))
            for stage in passes:
                number, _, where = come[1, stage]
                pass_on(
                    stage, get("own", stage), get("keep", stage), (get("come", number, 0), get("come", number, 1)), where,
                    out("total", stage), out("right"), out("left"), at[2, stage],
                )
            for stage in sums:
                number, _, where = come[2, stage]
                add_up(stage, get("total", stage), (get("come", number, 0), get("come", number, 1)), where, out("sum", stage))
            for n, (coded, *tiles) in enumerate(sends):
                for i, (first, second) in enumerate(tiles):
                    value = out("sum", first[0])[first[1]]
                    if first != second:
                        value = jnp.where(core == 0, value, out("sum", second[0])[second[1]])
                    if coded:
                        exponent = exponent_of(jnp.max(jnp.abs(value), axis=(0, 1), keepdims=True))
                        out("send", n)[i * QUARTER : (i + 1) * QUARTER, :] = encode(value, exponent)
                        put_exponent(out("send", n), len(tiles) * QUARTER, i, exponent)
                    else:
                        out("send", n)[i] = value
            for move in moves:
                move.wait()

        size = lambda a: a.size * a.dtype.itemsize
        depth = STAGES[pack_of] if pack_of else 1
        made = pl.pallas_call(
            kernel,
            out_shape=shapes,
            in_specs=[SMEM] + [VMEM] * len(arrays),
            out_specs=[VMEM] * len(shapes),
            scratch_shapes=[pltpu.VMEM((depth, BLOCK, BLOCK), F32), pltpu.SemaphoreType.DMA((max(1, len(copies)),))],
            compiler_params=pltpu.CompilerParams(vmem_limit_bytes=16 << 20),
            cost_estimate=pl.CostEstimate(
                flops=10**11, bytes_accessed=0, transcendentals=0
            ),
        )(self.place, *arrays)
        self.token = made[0]
        for key, n in outs.items():
            if key[0] in ("own", "keep", "total"):
                self.held[key] = made[n]
            if key[0] == "sum":
                self.sums[key[1]] = made[n]
        if sections:
            pair = tuple(
                lax.ppermute(made[outs[side]], "smp", [(i, (i + by) % 4) for i in range(4)])
                for side, by in (("right", 1), ("left", 3))
            )
            number = len(self.come)
            for section in sections:
                self.come[section] = (number, pair, at[section])
        return [made[n] for key, n in outs.items() if key[0] in ("copy", "send")]


def decoded(coded, count, tile):
    return decode(coded[tile * QUARTER : (tile + 1) * QUARTER, :], get_exponent(coded, count * QUARTER, tile))


def scaled(value, reach, rows, cols, block, offset, cut=slice(0, BLOCK)):
    inside = (offset <= reach[block]).astype(F32)
    product = (value * rows[block * QUARTER : (block + 1) * QUARTER, :]) * cols[
        block + offset : block + offset + 1, cut
    ]
    return jnp.where(inside > 0, product, 0.0)


def own_work(core, refs, acc):
    d = refs[0]
    tile(acc, 0, d, 0, d, 0)
    tile(acc, 1, d, 0, d, BLOCK)
    tile(acc, 2, d, BLOCK, d, BLOCK)


def four_rows(d, other):
    return enumerate(((d, 0), (d, BLOCK), (other, 0), (other, BLOCK)))


def b_work(core, refs, acc):
    d, other, h1 = refs

    @pl.when(core == 0)
    def _():
        for t, (rows, row) in four_rows(d, other):
            tile(acc, t, rows, row, h1, 0)

    @pl.when(core == 1)
    def _():
        for t in range(4):
            tile(acc, t, other, (t // 2) * BLOCK, d, (t % 2) * BLOCK)


def c_work(core, refs, acc):
    d, other, h1, h2, m1 = refs

    @pl.when(core == 0)
    def _():
        for t, (rows, row) in four_rows(d, other):
            tile(acc, t, rows, row, h2, 0)

    @pl.when(core == 1)
    def _():
        tile(acc, 0, h1, 0, d, BLOCK)
        tile(acc, 1, h2, 0, d, BLOCK)
        tile(acc, 2, h1, 0, m1, 0)
        tile(acc, 3, h2, 0, m1, 0)


def d_work(core, refs, acc):
    d, other, h3 = refs

    @pl.when(core == 0)
    def _():
        for t, (rows, row) in four_rows(d, other):
            narrow(acc, t // 2, (t % 2) * CUT, rows, row, h3)

    @pl.when(core == 1)
    def _():
        acc[...] = jnp.zeros_like(acc)


def e_work(core, refs, acc):
    d, other, h1, h3, h4, m2 = refs

    @pl.when(core == 0)
    def _():
        for t, (rows, row) in four_rows(d, other):
            narrow(acc, t // 2, (t % 2) * CUT, rows, row, h4)

    @pl.when(core == 1)
    def _():
        acc[0, 0:CUT, :] = dot_t(h3[...], d[BLOCK : 2 * BLOCK, :])
        acc[0, CUT:BLOCK, :] = dot_t(h4[...], d[BLOCK : 2 * BLOCK, :])
        tile(acc, 1, h1, 0, m2, 0)


def near_kernel(place, d, near, sem):
    copies = []
    for n in range(8):
        first = n * HALF
        source = d.at[pl.ds(pl.multiple_of(place[1] * BLOCK + first, HALF), HALF), :]
        copies.append(pltpu.make_async_copy(source, near.at[first : first + HALF, :], sem.at[n]))
        copies[-1].start()
    for copy in copies:
        copy.wait()


def most_kernel(place, reach, rows, cols, a, b, c, swapped, zc, out):
    core = place[1]

    def write(block, offset, value):
        out[block, offset] = scaled(value, reach, rows, cols, block, offset)

    write(0, 0, a[0])
    write(0, 1, a[1])
    write(1, 0, a[2])

    @pl.when(core == 0)
    def _():
        write(0, 2, swapped[0])
        write(0, 3, swapped[1])
        write(1, 1, swapped[2])
        write(1, 2, swapped[3])
        write(0, 4, b[0])
        write(1, 3, b[1])
        write(0, 5, c[0])
        write(1, 4, c[1])

    @pl.when(core == 1)
    def _():
        write(0, 2, swapped[0])
        write(1, 1, swapped[1])
        write(0, 3, swapped[2])
        write(1, 2, swapped[3])
        write(1, 4, decoded(zc, 4, 0))
        write(0, 5, decoded(zc, 4, 1))
        write(1, 5, decoded(zc, 4, 2))
        write(0, 6, decoded(zc, 4, 3))


def last_kernel(place, reach, rows, cols, d, e, crossed, edge, held, out, room, sem):
    del held
    core = place[1]
    sides = ((slice(0, CUT), 0), (slice(CUT, BLOCK), 1))

    def put(slot, block, offset, value, cut):
        room[slot, :, cut] = scaled(value, reach, rows, cols, block, offset, cut)

    def send(slot, block, offset):
        copy = pltpu.make_async_copy(room.at[slot], out.at[block, offset], sem.at[slot])
        copy.start()
        return copy

    @pl.when(core == 0)
    def _():
        copies = []
        for block, (at, _) in enumerate(sides):
            for (cut, _), held in zip(sides, (d, e)):
                put(block, block, 6 - block, held[0, :, at], cut)
            copies.append(send(block, block, 6 - block))
        put(2, 1, 6, decoded(crossed, 2, 0), slice(0, BLOCK))
        copies.append(send(2, 1, 6))
        for copy in copies:
            copy.wait()

    @pl.when(core == 1)
    def _():
        copies = []
        halves = [decoded(crossed, 2, side) for side in range(2)]
        for block, (at, _) in enumerate(sides):
            for cut, side in sides:
                put(block, block, 4 - block, halves[side][:, at], cut)
            copies.append(send(block, block, 4 - block))
        put(2, 1, 6, decoded(edge, 1, 0), slice(0, BLOCK))
        copies.append(send(2, 1, 6))
        for copy in copies:
            copy.wait()


def per_device(dosages, reach, counts):
    snp_size = lax.axis_size("snp")
    chips = snp_size // 2
    snp = lax.axis_index("snp")
    x = lax.axis_index("smp")
    core = lax.rem(snp, 2)
    place = jnp.stack([x, core]).astype(jnp.int32)

    def hop(v, *moves):
        pairs = [
            (2 * chip + source, 2 * (chip + by) + target)
            for chip in range(chips)
            for source, by, target in moves
            if 0 <= chip + by < chips
        ]
        return lax.ppermute(v, "snp", pairs)

    flops = lambda tiles: 2 * tiles * BLOCK * BLOCK * dosages.shape[1]
    net = Reduction(place)
    far = lambda more: lambda core: (1 - core) * BLOCK + more
    whole = lambda core: 0
    block_shape = jax.ShapeDtypeStruct((BLOCK, dosages.shape[1]), dosages.dtype)

    near = pl.pallas_call(
        near_kernel,
        out_shape=block_shape,
        in_specs=[SMEM, ANY],
        out_specs=VMEM,
        scratch_shapes=[pltpu.SemaphoreType.DMA((8,))],
    )(place, dosages)
    h1 = hop(near, (0, -1, 0), (1, 1, 1))
    other = hop(dosages, (0, 0, 1), (1, 0, 0))
    inv = lax.rsqrt(counts.astype(F32))
    inv = jnp.concatenate([inv, jnp.ones((REACH_MAX * BLOCK,), F32)])
    cols = lax.dynamic_slice_in_dim(inv, snp * 2 * BLOCK, 8 * BLOCK, 0).reshape(8, BLOCK)
    rows = lax.dynamic_slice_in_dim(cols[:2], x * QUARTER, QUARTER, 1).reshape(2 * QUARTER, 1)
    here = lax.dynamic_slice_in_dim(reach, snp * 2, 2, 0)
    (far2,) = net.step(
        own_work, [dosages, rows, cols], "a", sections=[(1, "a")], copies=[(BLOCK, 0, far(0))], flops=flops(3)
    )
    h2 = hop(far2, (0, -1, 0), (1, 1, 1))
    m1 = hop(h1, (0, 0, 1))
    (far3,) = net.step(
        b_work, [dosages, other, h1], "b", passes=["a"], sections=[(1, "b"), (2, "a")],
        copies=[(CUT, 0, far(0))], flops=flops(4),
    )
    h3 = hop(far3, (1, -1, 0), (0, 1, 1))
    far4, forward = net.step(
        c_work, [dosages, other, h1, h2, m1], "c", sections=[(1, "c")],
        copies=[(CUT, 0, far(CUT)), (BLOCK, 3, whole)], flops=flops(4),
    )
    h4 = hop(far4, (1, -1, 0), (0, 1, 1))
    m2 = hop(forward, (0, 0, 1))
    net.step(
        d_work, [dosages, other, h3], "d", passes=["b"], sums=["a"], sections=[(1, "d"), (2, "b")], flops=flops(2)
    )
    net.step(
        e_work, [dosages, other, h1, h3, h4, m2], "e", passes=["c"], sections=[(1, "e"), (2, "c")], flops=flops(2)
    )
    swapping, coded_c = net.step(
        passes=["d", "e"], sums=["b", "c"], sections=[(2, "d"), (2, "e")],
        sends=[
            (False, (("b", 2), ("b", 0)), (("b", 3), ("b", 1)), (("c", 2), ("b", 2)), (("c", 3), ("b", 3))),
            (True, *(((stage, t),) * 2 for stage, t in (("c", 0), ("c", 1), ("c", 2), ("c", 3)))),
        ],
    )
    swapped = hop(swapping, (0, 0, 1), (1, 0, 0))
    zc = hop(coded_c, (1, -1, 1))
    crossing, ending = net.step(
        sums=["d", "e"],
        sends=[(True, (("d", 1), ("e", 0)), (("e", 1), ("e", 1))), (True, (("e", 1), ("e", 1)))],
    )
    crossed = hop(crossing, (0, 0, 1), (1, -1, 0))
    edge = hop(ending, (1, -1, 1))
    out_shape = jax.ShapeDtypeStruct((2, REACH_MAX + 1, QUARTER, BLOCK), F32)
    s = net.sums
    parts = (rows, cols, s["a"], s["b"], s["c"], swapped, zc)
    out = pl.pallas_call(
        most_kernel,
        out_shape=out_shape,
        in_specs=[SMEM] * 2 + [VMEM] * len(parts),
        out_specs=VMEM,
        compiler_params=pltpu.CompilerParams(vmem_limit_bytes=16 << 20),
        cost_estimate=pl.CostEstimate(flops=10**11, bytes_accessed=0, transcendentals=0),
    )(place, here, *parts)
    return pl.pallas_call(
        last_kernel,
        out_shape=out_shape,
        in_specs=[SMEM] * 2 + [VMEM] * 6 + [ANY],
        out_specs=ANY,
        scratch_shapes=[pltpu.VMEM((3, QUARTER, BLOCK), F32), pltpu.SemaphoreType.DMA((3,))],
        input_output_aliases={8: 0},
        compiler_params=pltpu.CompilerParams(vmem_limit_bytes=8 << 20),
    )(place, here, rows, cols, s["d"], s["e"], crossed, edge, out)


def solution(mesh):
    in_specs = (P("snp", "smp"), P(), P())
    out_specs = P("snp", None, "smp", None)
    return jax.shard_map(
        per_device, mesh=mesh, in_specs=in_specs, out_specs=out_specs, check_vma=False
    )
```

```python
import functools

import jax
import jax.numpy as jnp
from jax import lax
from jax.experimental import pallas as pl
from jax.experimental.pallas import tpu as pltpu
from jax.sharding import PartitionSpec as P

BLOCK = 512
REACH_MAX = 6
QUARTER = 128
HALF = 64
TAIL = 16
CUT = 256
FULL = 32766.0
VMEM = pl.BlockSpec(memory_space=pltpu.VMEM)
SMEM = pl.BlockSpec(memory_space=pltpu.SMEM)
ANY = pl.BlockSpec(memory_space=pl.ANY)
F32 = jnp.float32
STAGES = {"a": 3, "b": 4, "c": 4, "d": 2, "e": 2}


def exponent_of(most):
    return jnp.clip(jnp.ceil(jnp.log2(jnp.maximum(most, 1e-30))), -100.0, 100.0)


def encode(value, exponent):
    part = jnp.maximum(jnp.abs(value) * (jnp.exp2(-exponent) * (FULL * FULL)), 1e-20)
    root = jnp.minimum(part * lax.rsqrt(part), FULL)
    root = (root + 0.5).astype(jnp.int32)
    return jnp.where(value < 0, -root, root).astype(jnp.int16)


def decode(code, exponent):
    root = code.astype(jnp.int32).astype(F32)
    return root * jnp.abs(root) * (jnp.exp2(exponent) * (1.0 / (FULL * FULL)))


def put_exponent(message, row, tile, exponent):
    message[row : row + TAIL, tile * 128 : tile * 128 + 128] = (
        jnp.broadcast_to(exponent, (TAIL, 128)).astype(jnp.int32).astype(jnp.int16)
    )


def get_exponent(message, row, tile):
    held = message[row : row + TAIL, tile * 128 : tile * 128 + 128]
    return jnp.max(held.astype(jnp.int32).astype(F32), axis=(0, 1), keepdims=True)


def section_rows(section):
    part, stage = section
    return STAGES[stage] * (QUARTER if part == 1 else HALF)


def layout(sections):
    first, places = 0, {}
    for section in sections:
        places[section] = first
        first += section_rows(section)
    return {s: (at, first + TAIL * n) for n, (s, at) in enumerate(places.items())}, first + TAIL * len(sections)


def pack(stage, x, acc, right, left, at, own, keep):
    def quarter(steps, half):
        return pl.multiple_of(lax.rem(x + steps, 4) * QUARTER + half * HALF, HALF)

    for t in range(STAGES[stage]):
        most = jnp.zeros((TAIL, BLOCK), F32)
        for first in range(0, BLOCK, TAIL):
            most = jnp.maximum(most, jnp.abs(acc[t, first : first + TAIL, :]))
        exponent = exponent_of(jnp.max(most, axis=(0, 1), keepdims=True))

        def rows_of(steps, half):
            return acc[t, pl.ds(quarter(steps, half), HALF), :]

        base = at[0] + t * QUARTER
        for half in range(2):
            own[t, half * HALF : (half + 1) * HALF, :] = rows_of(0, half)
        right[base : base + HALF, :] = encode(rows_of(2, 0), exponent)
        right[base + HALF : base + QUARTER, :] = encode(rows_of(1, 1), exponent)
        left[base : base + HALF, :] = encode(rows_of(2, 1), exponent)
        left[base + HALF : base + QUARTER, :] = encode(rows_of(3, 0), exponent)
        keep[t, 0:HALF, :] = rows_of(1, 0)
        keep[t, HALF:QUARTER, :] = rows_of(3, 1)
        put_exponent(right, at[1], t, exponent)
        put_exponent(left, at[1], t, exponent)


def pass_on(stage, own, keep, come, come_at, total, right, left, at):
    from_left, from_right = come
    for t in range(STAGES[stage]):
        base = come_at[0] + t * QUARTER
        left_exp = get_exponent(from_left, come_at[1], t)
        right_exp = get_exponent(from_right, come_at[1], t)
        total[t, HALF:QUARTER, :] = own[t, HALF:QUARTER, :] + decode(
            from_left[base + HALF : base + QUARTER, :], left_exp
        )
        total[t, 0:HALF, :] = own[t, 0:HALF, :] + decode(
            from_right[base + HALF : base + QUARTER, :], right_exp
        )
        to_right = keep[t, 0:HALF, :] + decode(from_left[base : base + HALF, :], left_exp)
        to_left = keep[t, HALF:QUARTER, :] + decode(from_right[base : base + HALF, :], right_exp)
        first = at[0] + t * HALF
        for message, value in ((right, to_right), (left, to_left)):
            exponent = exponent_of(jnp.max(jnp.abs(value), axis=(0, 1), keepdims=True))
            message[first : first + HALF, :] = encode(value, exponent)
            put_exponent(message, at[1], t, exponent)


def add_up(stage, total, come, come_at, out):
    from_left, from_right = come
    for t in range(STAGES[stage]):
        first = come_at[0] + t * HALF
        out[t, 0:HALF, :] = total[t, 0:HALF, :] + decode(
            from_left[first : first + HALF, :], get_exponent(from_left, come_at[1], t)
        )
        out[t, HALF:QUARTER, :] = total[t, HALF:QUARTER, :] + decode(
            from_right[first : first + HALF, :], get_exponent(from_right, come_at[1], t)
        )


def dot_t(a, b):
    return lax.dot_general(a, b, (((1,), (1,)), ((), ())), preferred_element_type=F32)


def tile(acc, t, rows, row, cols, col):
    acc[t] = dot_t(rows[row : row + BLOCK, :], cols[col : col + BLOCK, :])


def narrow(acc, t, col, rows, row, cols):
    acc[t, :, col : col + CUT] = dot_t(rows[row : row + BLOCK, :], cols[...])


class Reduction:
    def __init__(self, place):
        self.place = place
        self.held, self.come, self.sums = {}, {}, {}
        self.token = jnp.zeros((8, 128), F32)

    def step(self, work=None, operands=(), pack_of=None, passes=(), sums=(), sections=(), copies=(), sends=(), flops=0):
        arrays, places = [], {}

        def take(key, value):
            if key not in places:
                places[key] = len(arrays)
                arrays.append(value)

        for n, operand in enumerate(operands):
            take(("operand", n), operand)
        for stage in passes:
            take(("own", stage), self.held["own", stage])
            take(("keep", stage), self.held["keep", stage])
        for stage in sums:
            take(("total", stage), self.held["total", stage])
        take(("token",), self.token)
        come = dict(self.come)
        for source in [(1, s) for s in passes] + [(2, s) for s in sums]:
            number, pair, _ = come[source]
            take(("come", number, 0), pair[0])
            take(("come", number, 1), pair[1])
        outs, shapes = {}, []

        def give(key, shape, dtype=F32):
            outs[key] = len(shapes)
            shapes.append(jax.ShapeDtypeStruct(shape, dtype))

        give(("token",), (8, 128))
        at, rows = layout(sections)
        if sections:
            give("right", (rows, BLOCK), jnp.int16)
            give("left", (rows, BLOCK), jnp.int16)
        if pack_of:
            give(("own", pack_of), (STAGES[pack_of], QUARTER, BLOCK))
            give(("keep", pack_of), (STAGES[pack_of], QUARTER, BLOCK))
        for stage in passes:
            give(("total", stage), (STAGES[stage], QUARTER, BLOCK))
        for stage in sums:
            give(("sum", stage), (STAGES[stage], QUARTER, BLOCK))
        for n, (coded, *tiles) in enumerate(sends):
            if coded:
                give(("send", n), (len(tiles) * QUARTER + TAIL, BLOCK), jnp.int16)
            else:
                give(("send", n), (len(tiles), QUARTER, BLOCK))
        for n, (count, operand, _) in enumerate(copies):
            give(("copy", n), (count, operands[operand].shape[1]), operands[operand].dtype)

        def kernel(place, *refs):
            ins, made = refs[: len(arrays)], refs[len(arrays) : len(arrays) + len(shapes)]
            acc, sems = refs[-2:]
            x, core = place[0], place[1]
            made[0][...] = ins[places[("token",)]][...]
            get = lambda *key: ins[places[key]]
            out = lambda *key: made[outs[key if len(key) > 1 else key[0]]]
            moves = []
            for n, (count, operand, first) in enumerate(copies):
                source = ins[operand].at[pl.ds(pl.multiple_of(first(core), CUT), count), :]
                moves.append(pltpu.make_async_copy(source, out("copy", n), sems.at[n]))
                moves[-1].start()
            if work is not None:
                work(core, ins[: len(operands)], acc)
            if pack_of:
                pack(pack_of, x, acc, out("right"), out("left"), at[1, pack_of], out("own", pack_of), out("keep", pack_of))
            for stage in passes:
                number, _, where = come[1, stage]
                pass_on(
                    stage, get("own", stage), get("keep", stage), (get("come", number, 0), get("come", number, 1)), where,
                    out("total", stage), out("right"), out("left"), at[2, stage],
                )
            for stage in sums:
                number, _, where = come[2, stage]
                add_up(stage, get("total", stage), (get("come", number, 0), get("come", number, 1)), where, out("sum", stage))
            for n, (coded, *tiles) in enumerate(sends):
                for i, (first, second) in enumerate(tiles):
                    value = out("sum", first[0])[first[1]]
                    if first != second:
                        value = jnp.where(core == 0, value, out("sum", second[0])[second[1]])
                    if coded:
                        exponent = exponent_of(jnp.max(jnp.abs(value), axis=(0, 1), keepdims=True))
                        out("send", n)[i * QUARTER : (i + 1) * QUARTER, :] = encode(value, exponent)
                        put_exponent(out("send", n), len(tiles) * QUARTER, i, exponent)
                    else:
                        out("send", n)[i] = value
            for move in moves:
                move.wait()

        size = lambda a: a.size * a.dtype.itemsize
        depth = STAGES[pack_of] if pack_of else 1
        made = pl.pallas_call(
            kernel,
            out_shape=shapes,
            in_specs=[SMEM] + [VMEM] * len(arrays),
            out_specs=[VMEM] * len(shapes),
            scratch_shapes=[pltpu.VMEM((depth, BLOCK, BLOCK), F32), pltpu.SemaphoreType.DMA((max(1, len(copies)),))],
            compiler_params=pltpu.CompilerParams(vmem_limit_bytes=16 << 20),
            cost_estimate=pl.CostEstimate(
                flops=10**11, bytes_accessed=0, transcendentals=0
            ),
        )(self.place, *arrays)
        self.token = made[0]
        for key, n in outs.items():
            if key[0] in ("own", "keep", "total"):
                self.held[key] = made[n]
            if key[0] == "sum":
                self.sums[key[1]] = made[n]
        if sections:
            pair = tuple(
                lax.ppermute(made[outs[side]], "smp", [(i, (i + by) % 4) for i in range(4)])
                for side, by in (("right", 1), ("left", 3))
            )
            number = len(self.come)
            for section in sections:
                self.come[section] = (number, pair, at[section])
        return [made[n] for key, n in outs.items() if key[0] in ("copy", "send")]


def decoded(coded, count, tile):
    return decode(coded[tile * QUARTER : (tile + 1) * QUARTER, :], get_exponent(coded, count * QUARTER, tile))


def scaled(value, reach, rows, cols, block, offset, cut=slice(0, BLOCK)):
    inside = (offset <= reach[block]).astype(F32)
    product = (value * rows[block * QUARTER : (block + 1) * QUARTER, :]) * cols[
        block + offset : block + offset + 1, cut
    ]
    return jnp.where(inside > 0, product, 0.0)


def own_work(core, refs, acc):
    d = refs[0]
    tile(acc, 0, d, 0, d, 0)
    tile(acc, 1, d, 0, d, BLOCK)
    tile(acc, 2, d, BLOCK, d, BLOCK)


def four_rows(d, other):
    return enumerate(((d, 0), (d, BLOCK), (other, 0), (other, BLOCK)))


def b_work(core, refs, acc):
    d, other, h1 = refs

    @pl.when(core == 0)
    def _():
        for t, (rows, row) in four_rows(d, other):
            tile(acc, t, rows, row, h1, 0)

    @pl.when(core == 1)
    def _():
        for t in range(4):
            tile(acc, t, other, (t // 2) * BLOCK, d, (t % 2) * BLOCK)


def c_work(core, refs, acc):
    d, other, h1, h2, m1 = refs

    @pl.when(core == 0)
    def _():
        for t, (rows, row) in four_rows(d, other):
            tile(acc, t, rows, row, h2, 0)

    @pl.when(core == 1)
    def _():
        tile(acc, 0, h1, 0, d, BLOCK)
        tile(acc, 1, h2, 0, d, BLOCK)
        tile(acc, 2, h1, 0, m1, 0)
        tile(acc, 3, h2, 0, m1, 0)


def d_work(core, refs, acc):
    d, other, h3 = refs

    @pl.when(core == 0)
    def _():
        for t, (rows, row) in four_rows(d, other):
            narrow(acc, t // 2, (t % 2) * CUT, rows, row, h3)

    @pl.when(core == 1)
    def _():
        acc[...] = jnp.zeros_like(acc)


def e_work(core, refs, acc):
    d, other, h1, h3, h4, m2 = refs

    @pl.when(core == 0)
    def _():
        for t, (rows, row) in four_rows(d, other):
            narrow(acc, t // 2, (t % 2) * CUT, rows, row, h4)

    @pl.when(core == 1)
    def _():
        acc[0, 0:CUT, :] = dot_t(h3[...], d[BLOCK : 2 * BLOCK, :])
        acc[0, CUT:BLOCK, :] = dot_t(h4[...], d[BLOCK : 2 * BLOCK, :])
        tile(acc, 1, h1, 0, m2, 0)


def near_kernel(place, d, near, sem):
    copies = []
    for n in range(8):
        first = n * HALF
        source = d.at[pl.ds(pl.multiple_of(place[1] * BLOCK + first, HALF), HALF), :]
        copies.append(pltpu.make_async_copy(source, near.at[first : first + HALF, :], sem.at[n]))
        copies[-1].start()
    for copy in copies:
        copy.wait()


def most_kernel(place, reach, rows, cols, a, b, c, swapped, zc, out):
    core = place[1]

    def write(block, offset, value):
        out[block, offset] = scaled(value, reach, rows, cols, block, offset)

    write(0, 0, a[0])
    write(0, 1, a[1])
    write(1, 0, a[2])

    @pl.when(core == 0)
    def _():
        write(0, 2, swapped[0])
        write(0, 3, swapped[1])
        write(1, 1, swapped[2])
        write(1, 2, swapped[3])
        write(0, 4, b[0])
        write(1, 3, b[1])
        write(0, 5, c[0])
        write(1, 4, c[1])

    @pl.when(core == 1)
    def _():
        write(0, 2, swapped[0])
        write(1, 1, swapped[1])
        write(0, 3, swapped[2])
        write(1, 2, swapped[3])
        write(1, 4, decoded(zc, 4, 0))
        write(0, 5, decoded(zc, 4, 1))
        write(1, 5, decoded(zc, 4, 2))
        write(0, 6, decoded(zc, 4, 3))


def last_kernel(place, reach, rows, cols, d, e, crossed, edge, held, out, room, sem):
    del held
    core = place[1]
    sides = ((slice(0, CUT), 0), (slice(CUT, BLOCK), 1))

    def put(slot, block, offset, value, cut):
        room[slot, :, cut] = scaled(value, reach, rows, cols, block, offset, cut)

    def send(slot, block, offset):
        copy = pltpu.make_async_copy(room.at[slot], out.at[block, offset], sem.at[slot])
        copy.start()
        return copy

    @pl.when(core == 0)
    def _():
        copies = []
        for block, (at, _) in enumerate(sides):
            for (cut, _), held in zip(sides, (d, e)):
                put(block, block, 6 - block, held[0, :, at], cut)
            copies.append(send(block, block, 6 - block))
        put(2, 1, 6, decoded(crossed, 2, 0), slice(0, BLOCK))
        copies.append(send(2, 1, 6))
        for copy in copies:
            copy.wait()

    @pl.when(core == 1)
    def _():
        copies = []
        halves = [decoded(crossed, 2, side) for side in range(2)]
        for block, (at, _) in enumerate(sides):
            for cut, side in sides:
                put(block, block, 4 - block, halves[side][:, at], cut)
            copies.append(send(block, block, 4 - block))
        put(2, 1, 6, decoded(edge, 1, 0), slice(0, BLOCK))
        copies.append(send(2, 1, 6))
        for copy in copies:
            copy.wait()


def per_device(dosages, reach, counts):
    snp_size = lax.axis_size("snp")
    chips = snp_size // 2
    snp = lax.axis_index("snp")
    x = lax.axis_index("smp")
    core = lax.rem(snp, 2)
    place = jnp.stack([x, core]).astype(jnp.int32)

    def hop(v, *moves):
        pairs = [
            (2 * chip + source, 2 * (chip + by) + target)
            for chip in range(chips)
            for source, by, target in moves
            if 0 <= chip + by < chips
        ]
        return lax.ppermute(v, "snp", pairs)

    flops = lambda tiles: 2 * tiles * BLOCK * BLOCK * dosages.shape[1]
    net = Reduction(place)
    far = lambda more: lambda core: (1 - core) * BLOCK + more
    whole = lambda core: 0
    block_shape = jax.ShapeDtypeStruct((BLOCK, dosages.shape[1]), dosages.dtype)

    near = pl.pallas_call(
        near_kernel,
        out_shape=block_shape,
        in_specs=[SMEM, ANY],
        out_specs=VMEM,
        scratch_shapes=[pltpu.SemaphoreType.DMA((8,))],
    )(place, dosages)
    h1 = hop(near, (0, -1, 0), (1, 1, 1))
    other = hop(dosages, (0, 0, 1), (1, 0, 0))
    inv = lax.rsqrt(counts.astype(F32))
    inv = jnp.concatenate([inv, jnp.ones((REACH_MAX * BLOCK,), F32)])
    cols = lax.dynamic_slice_in_dim(inv, snp * 2 * BLOCK, 8 * BLOCK, 0).reshape(8, BLOCK)
    rows = lax.dynamic_slice_in_dim(cols[:2], x * QUARTER, QUARTER, 1).reshape(2 * QUARTER, 1)
    here = lax.dynamic_slice_in_dim(reach, snp * 2, 2, 0)
    (far2,) = net.step(
        own_work, [dosages, rows, cols], "a", sections=[(1, "a")], copies=[(BLOCK, 0, far(0))], flops=flops(3)
    )
    h2 = hop(far2, (0, -1, 0), (1, 1, 1))
    m1 = hop(h1, (0, 0, 1))
    (far3,) = net.step(
        b_work, [dosages, other, h1], "b", passes=["a"], sections=[(1, "b"), (2, "a")],
        copies=[(CUT, 0, far(0))], flops=flops(4),
    )
    h3 = hop(far3, (1, -1, 0), (0, 1, 1))
    far4, forward = net.step(
        c_work, [dosages, other, h1, h2, m1], "c", sections=[(1, "c")],
        copies=[(CUT, 0, far(CUT)), (BLOCK, 3, whole)], flops=flops(4),
    )
    h4 = hop(far4, (1, -1, 0), (0, 1, 1))
    m2 = hop(forward, (0, 0, 1))
    net.step(
        d_work, [dosages, other, h3], "d", passes=["b"], sums=["a"], sections=[(1, "d"), (2, "b")], flops=flops(2)
    )
    net.step(
        e_work, [dosages, other, h1, h3, h4, m2], "e", sections=[(1, "e")], flops=flops(2)
    )
    net.step(passes=["c"], sections=[(2, "c")])
    net.step(passes=["d", "e"], sections=[(2, "d"), (2, "e")])
    swapping, coded_c = net.step(
        sums=["b", "c"],
        sends=[
            (False, (("b", 2), ("b", 0)), (("b", 3), ("b", 1)), (("c", 2), ("b", 2)), (("c", 3), ("b", 3))),
            (True, *(((stage, t),) * 2 for stage, t in (("c", 0), ("c", 1), ("c", 2), ("c", 3)))),
        ],
    )
    swapped = hop(swapping, (0, 0, 1), (1, 0, 0))
    zc = hop(coded_c, (1, -1, 1))
    crossing, ending = net.step(
        sums=["d", "e"],
        sends=[(True, (("d", 1), ("e", 0)), (("e", 1), ("e", 1))), (True, (("e", 1), ("e", 1)))],
    )
    crossed = hop(crossing, (0, 0, 1), (1, -1, 0))
    edge = hop(ending, (1, -1, 1))
    out_shape = jax.ShapeDtypeStruct((2, REACH_MAX + 1, QUARTER, BLOCK), F32)
    s = net.sums
    parts = (rows, cols, s["a"], s["b"], s["c"], swapped, zc)
    out = pl.pallas_call(
        most_kernel,
        out_shape=out_shape,
        in_specs=[SMEM] * 2 + [VMEM] * len(parts),
        out_specs=VMEM,
        compiler_params=pltpu.CompilerParams(vmem_limit_bytes=16 << 20),
        cost_estimate=pl.CostEstimate(flops=10**11, bytes_accessed=0, transcendentals=0),
    )(place, here, *parts)
    return pl.pallas_call(
        last_kernel,
        out_shape=out_shape,
        in_specs=[SMEM] * 2 + [VMEM] * 6 + [ANY],
        out_specs=ANY,
        scratch_shapes=[pltpu.VMEM((3, QUARTER, BLOCK), F32), pltpu.SemaphoreType.DMA((3,))],
        input_output_aliases={8: 0},
        compiler_params=pltpu.CompilerParams(vmem_limit_bytes=8 << 20),
    )(place, here, rows, cols, s["d"], s["e"], crossed, edge, out)


def solution(mesh):
    in_specs = (P("snp", "smp"), P(), P())
    out_specs = P("snp", None, "smp", None)
    return jax.shard_map(
        per_device, mesh=mesh, in_specs=in_specs, out_specs=out_specs, check_vma=False
    )
```
